32 devices in a mesh: hi: 4 (over y, core), lo: 8 (over z, x).
Axes of the slice: x: 2, y: 2, z: 4, core: 2. Of those that a mesh axis runs over, the one named last changes fastest.
Arguments:
- vectors: bfloat16 [128, 65536], P(None, ('hi', 'lo')), may hold values from -6 to 6
- leaves: bfloat16 [65536, 512], P(('hi', 'lo')), may hold values from -0.25 to 0.25
- u_local: bfloat16 [2, 65536, 128], P(None, ('hi', 'lo')), may hold values from -0.5 to 0.5
- v_local: bfloat16 [2, 65536, 128], P(None, ('hi', 'lo')), may hold values from -6 to 6
- u_upper: bfloat16 [5, 65536, 128], P(None, ('hi', 'lo')), may hold values from -0.5 to 0.5
- v_upper: bfloat16 [5, 65536, 128], P(None, ('hi', 'lo')), may hold values from -6 to 6
Outputs:
- krylov_last: bfloat16 [128, 65536], P(None, ('hi', 'lo'))
The draws below stay inside these ranges and needn't reach their ends.
All inputs are finite; a program needn't handle non-finite values.
Results may differ from the reference program's by a relative error of at most 0.018.
Values sent between devices are 32-bit elements; how exact they have to be, the bound alone decides.
A program may use at most 64 MiB of HBM per device.

```python
import math
import jax
import jax.numpy as jnp

LEAF = 512
RANK = 128
RHS = 128
LOCAL_LEVELS = 2
ITERS = 4
DIST_LEVELS = 5
NROWS = 65536


def shard_levels(stream_key, dims, shards, low, top_value):
    def one(axis_at, shards_of):
        steps = jax.random.uniform(jax.random.fold_in(jax.random.fold_in(stream_key, 6), axis_at), (shards_of,), jnp.float32, low / len(shards), top_value / len(shards))
        return jnp.repeat(jnp.exp(steps), dims[axis_at] // shards_of).reshape((-1,) + (1,) * (len(dims) - axis_at - 1))

    gain = one(*shards[0])
    for cut in shards[1:]:
        gain = gain * one(*cut)
    return gain


def centred(own_key, shape, spread, reach, cuts=(), kind=jnp.bfloat16):
    values = spread * jax.random.normal(own_key, shape, jnp.float32)
    if cuts:
        values = values * shard_levels(own_key, shape, cuts, -0.22, 0.18)
    return jnp.clip(values, -reach, reach).astype(kind)


def setup_inputs(seed: int = 0) -> dict:
    splits = jax.random.split(jax.random.key(seed), 7)
    vectors = centred(splits[0], (RHS, NROWS), 1.0, 6.0, ((1, 32),))
    leaves = centred(splits[1], (NROWS, LEAF), LEAF ** -0.5, 0.25, ((0, 32),))
    u_local = centred(splits[2], (LOCAL_LEVELS, NROWS, RANK), RANK ** -0.5, 0.5, ((1, 32),))
    v_local = centred(splits[3], (LOCAL_LEVELS, NROWS, RANK), 1.0, 6.0, ((1, 32),))
    u_upper = centred(splits[4], (DIST_LEVELS, NROWS, RANK), RANK ** -0.5, 0.5, ((1, 32),))
    v_upper = centred(splits[5], (DIST_LEVELS, NROWS, RANK), 1.0, 6.0, ((1, 32),))
    return {"vectors": vectors, "leaves": leaves, "u_local": u_local, "v_local": v_local, "u_upper": u_upper, "v_upper": v_upper}


def level_factors(level, u_local, v_local, u_upper, v_upper):
    if level < LOCAL_LEVELS:
        return (u_local[level], v_local[level])
    return (u_upper[level - LOCAL_LEVELS], v_upper[level - LOCAL_LEVELS])

def apply_operator(state, leaves, u_local, v_local, u_upper, v_upper):
    total_rows = state.shape[1]
    wide = state.shape[0]
    state_f = state.astype(jnp.float32)
    blocks = leaves.reshape(total_rows // LEAF, LEAF, LEAF).astype(jnp.float32)
    result = jnp.einsum('gij,cgj->cgi', blocks, state_f.reshape(wide, total_rows // LEAF, LEAF))
    result = result.reshape(wide, total_rows)
    level_count = LOCAL_LEVELS + DIST_LEVELS
    for level in range(level_count):
        u_mat, v_mat = level_factors(level, u_local, v_local, u_upper, v_upper)
        node_rows = LEAF * 2 ** level
        groups = total_rows // node_rows
        coef = jnp.einsum('gsr,cgs->gcr', v_mat.astype(jnp.float32).reshape(groups, node_rows, RANK), state_f.reshape(wide, groups, node_rows))
        coef = coef.reshape(groups // 2, 2, wide, RANK)[:, ::-1].reshape(groups, wide, RANK)
        coef = (coef * (1.0 / math.sqrt(node_rows * level_count))).astype(jnp.bfloat16)
        added = jnp.einsum('gsr,gcr->cgs', u_mat.astype(jnp.float32).reshape(groups, node_rows, RANK), coef.astype(jnp.float32))
        result = result + added.reshape(wide, total_rows)
    return result.astype(jnp.bfloat16)

def reference(vectors, leaves, u_local, v_local, u_upper, v_upper):
    state = vectors
    for step in range(ITERS):
        state = apply_operator(state, leaves, u_local, v_local, u_upper, v_upper)
    return state
```

```python
import functools
import math

import jax
import jax.numpy as jnp
from jax import lax
from jax.experimental import pallas as pl
from jax.experimental.pallas import tpu as pltpu
from jax.sharding import PartitionSpec as P

ITERS = 4
GROUP_BITS = 3
CHUNKS = 1
MESH = pl.DeviceIdType.MESH
F32 = jnp.float32
BF16 = jnp.bfloat16


def flip(value, mask):
    bit = 0
    out = value
    while mask >> bit:
        if (mask >> bit) & 1:
            step = 2**bit
            out = out + step - 2 * step * lax.rem(lax.div(value, step), 2)
        bit += 1
    return out


class Plan:
    def __init__(self, levels, group_bits, wide):
        self.levels = levels
        self.k = min(group_bits, levels - 1)
        self.wide = wide
        k = self.k
        self.runs = [(b, 1, 2**b) for b in range(1, k)] + [(k, levels - k, 2**k)]
        self.first = [(r, m) for r, run in enumerate(self.runs) for m in range(1, run[2])]
        self.cross = [(b, m) for b in range(levels) for m in range(2 ** max(0, b - k))]
        self.slots2 = [(b, m) for b, m in self.cross if b > k]

    def rows(self, group):
        return self.wide // group

    def cross_mask(self, b, m):
        return (1 << b) ^ (m << self.k)

    def partners(self):
        masks = {m for _, m in self.first} | {self.cross_mask(b, m) for b, m in self.cross}
        return sorted(masks)


def nt(a, b):
    return lax.dot_general(a, b, (((1,), (1,)), ((), ())), preferred_element_type=F32)


def nn(a, b):
    return jnp.dot(a, b, preferred_element_type=F32)


def kernel(plan, lo_size, chunks, leaf_rows, *refs):
    hbm, o_ref = refs[:6], refs[6]
    leaves, u_loc, v_loc, u_up, v_up = refs[7:12]
    acc, parts, coef, recv2 = refs[12:16]
    recv1 = refs[16 : 16 + len(plan.runs)]
    load_sem, s1, r1, s2, r2, s3, r3 = refs[16 + len(plan.runs) :]
    levels, k = plan.levels, plan.k
    wide = plan.wide
    dev_rows = o_ref.shape[1]
    local_count = u_loc.shape[0]
    level_count = local_count + levels
    leaf_count = dev_rows // leaf_rows
    lo_bits = lo_size.bit_length() - 1

    dests = (o_ref, leaves, u_loc, v_loc, u_up, v_up)
    loads = [pltpu.make_async_copy(hbm[i], dests[i], load_sem.at[i]) for i in range(6)]
    for i in (0, 5, 1, 3, 2, 4):
        loads[i].start()

    hi = lax.axis_index("hi")
    lo = lax.axis_index("lo")
    me = hi * lo_size + lo

    def peer(mask):
        return (flip(hi, mask >> lo_bits), flip(lo, mask & (lo_size - 1)))

    barrier = pltpu.get_barrier_semaphore()
    masks = plan.partners()
    for mask in masks:
        pl.semaphore_signal(barrier, inc=1, device_id=peer(mask), device_id_type=MESH)
    loads[0].wait()
    loads[5].wait()
    pl.semaphore_wait(barrier, len(masks))

    def piece(group, mask):
        rows = plan.rows(group)
        index = flip(lax.rem(me, group), mask)
        return pl.ds(pl.multiple_of(index * rows, 8), rows)

    def copy1(slot, i):
        run, m = plan.first[i]
        b, count, group = plan.runs[run]
        return pltpu.make_async_remote_copy(
            src_ref=parts.at[slot, pl.ds(b, count), piece(group, m)],
            dst_ref=recv1[run].at[slot, m - 1],
            send_sem=s1.at[slot, i],
            recv_sem=r1.at[slot, i],
            device_id=peer(m),
            device_id_type=MESH,
        )

    def copy2(slot, i):
        b, m = plan.cross[i]
        mine = piece(2 ** min(b, k), 0)
        if b > k:
            target = recv2.at[slot, plan.slots2.index((b, m))]
        else:
            target = coef.at[slot, b, mine]
        return pltpu.make_async_remote_copy(
            src_ref=parts.at[slot, b, mine],
            dst_ref=target,
            send_sem=s2.at[slot, i],
            recv_sem=r2.at[slot, i],
            device_id=peer(plan.cross_mask(b, m)),
            device_id_type=MESH,
        )

    def copy3(slot, i):
        run, m = plan.first[i]
        b, count, group = plan.runs[run]
        mine = coef.at[slot, pl.ds(b, count), piece(group, 0)]
        return pltpu.make_async_remote_copy(
            src_ref=mine,
            dst_ref=mine,
            send_sem=s3.at[slot, i],
            recv_sem=r3.at[slot, i],
            device_id=peer(m),
            device_id_type=MESH,
        )

    def factor(node_rows):
        return 1.0 / math.sqrt(node_rows * level_count)

    def leaf_slice(g):
        return slice(g * leaf_rows, (g + 1) * leaf_rows)

    def project(slot, c):
        me_rows = slice(c * wide, (c + 1) * wide)
        top = levels
        while top > 0:
            low = max(top - 2, 0)
            group = list(range(low, top))
            total = None
            for g in range(leaf_count):
                cols = leaf_slice(g)
                weights = jnp.concatenate([v_up[b, cols, :] for b in group], axis=1)
                term = nn(o_ref[me_rows, cols], weights)
                total = term if total is None else total + term
            rank = total.shape[1] // len(group)
            for i, b in enumerate(group):
                parts[slot, b] = total[:, i * rank : (i + 1) * rank]
            for i, (run, m) in enumerate(plan.first):
                if low <= plan.runs[run][0] < top:
                    copy1(slot, i).start()
            top = low
        for i, (b, m) in enumerate(plan.cross):
            if b == 0:
                copy2(slot, i).start()

    def local_part(slot, c):
        me_rows = slice(c * wide, (c + 1) * wide)
        sums = []
        for g in range(leaf_count):
            cols = leaf_slice(g)
            weights = jnp.concatenate([v_loc[j, cols, :] for j in range(local_count)], axis=1)
            sums.append(nn(o_ref[me_rows, cols], weights))
        rank = sums[0].shape[1] // local_count
        for g in range(leaf_count):
            cols = leaf_slice(g)
            pieces = []
            for j in range(local_count):
                node = (g >> j) ^ 1
                total = None
                for h in range(node << j, (node + 1) << j):
                    term = sums[h][:, j * rank : (j + 1) * rank]
                    total = term if total is None else total + term
                pieces.append((total * factor(leaf_rows * 2**j)).astype(BF16))
            bases = jnp.concatenate([u_loc[j, cols, :] for j in range(local_count)], axis=1)
            acc[me_rows, cols] = nt(o_ref[me_rows, cols], leaves[cols, :]) + nt(
                jnp.concatenate(pieces, axis=1), bases
            )

    def reduce_send(slot):
        for run, (b, count, group) in enumerate(plan.runs):
            for i, (r, m) in enumerate(plan.first):
                if r == run:
                    copy1(slot, i).wait_recv()
            mine = piece(group, 0)
            total = parts[slot, pl.ds(b, count), mine, :]
            for m in range(1, group):
                total = total + recv1[run][slot, m - 1]
            parts[slot, pl.ds(b, count), mine, :] = total
            for i, (level, m) in enumerate(plan.cross):
                if b <= level < b + count:
                    copy2(slot, i).start()

    def cross_send(slot):
        for run, (b, count, group) in enumerate(plan.runs):
            for level in range(b, b + count):
                total = None
                for i, (other, m) in enumerate(plan.cross):
                    if other == level:
                        copy2(slot, i).wait_recv()
                        if level > k:
                            term = recv2[slot, plan.slots2.index((level, m))]
                            total = term if total is None else total + term
                if total is not None:
                    coef[slot, level, piece(group, 0), :] = total
            for i, (r, m) in enumerate(plan.first):
                if r == run:
                    copy3(slot, i).start()

    def finish(slot, c):
        me_rows = slice(c * wide, (c + 1) * wide)
        for i, (b, m) in enumerate(plan.cross):
            if b == 0:
                copy2(slot, i).wait_recv()
        for i in range(len(plan.first)):
            copy3(slot, i).wait_recv()
        scaled = jnp.concatenate(
            [(coef[slot, b] * factor(dev_rows * 2**b)).astype(BF16) for b in range(levels)],
            axis=1,
        )
        for g in range(leaf_count):
            cols = leaf_slice(g)
            bases = jnp.concatenate([u_up[b, cols, :] for b in range(levels)], axis=1)
            o_ref[me_rows, cols] = (acc[me_rows, cols] + nt(scaled, bases)).astype(BF16)
        for i in range(len(plan.first)):
            copy1(slot, i).wait_send()
            copy3(slot, i).wait_send()
        for i in range(len(plan.cross)):
            copy2(slot, i).wait_send()

    def body(it, carry):
        slots = [it * chunks + c for c in range(chunks)]
        for c in range(chunks):
            project(slots[c], c)

        @pl.when(it == 0)
        def _():
            for i in (1, 2, 3):
                loads[i].wait()

        for c in range(chunks):
            local_part(slots[c], c)
            reduce_send(slots[c])
        for c in range(chunks):
            cross_send(slots[c])

        @pl.when(it == 0)
        def _():
            loads[4].wait()

        for c in range(chunks):
            finish(slots[c], c)
        return carry

    lax.fori_loop(0, ITERS, body, 0)


def local(vectors, leaves, u_local, v_local, u_upper, v_upper):
    wide = vectors.shape[0]
    levels = u_upper.shape[0]
    rank = u_upper.shape[2]
    plan = Plan(levels, GROUP_BITS, wide // CHUNKS)
    slots = ITERS * CHUNKS
    n1, n2 = len(plan.first), len(plan.cross)
    big = plan.rows(2**plan.k)
    dma = pltpu.SemaphoreType.DMA
    scratch = [pltpu.VMEM(x.shape, x.dtype) for x in (leaves, u_local, v_local, u_upper, v_upper)]
    scratch += [
        pltpu.VMEM(vectors.shape, F32),
        pltpu.VMEM((slots, levels, plan.wide, rank), F32),
        pltpu.VMEM((slots, levels, plan.wide, rank), F32),
        pltpu.VMEM((slots, max(1, len(plan.slots2)), big, rank), F32),
    ]
    scratch += [
        pltpu.VMEM((slots, group - 1, count, plan.rows(group), rank), F32)
        for _, count, group in plan.runs
    ]
    scratch += [dma((6,)), dma((slots, n1)), dma((slots, n1)), dma((slots, n2)), dma((slots, n2))]
    scratch += [dma((slots, n1)), dma((slots, n1))]
    return pl.pallas_call(
        functools.partial(kernel, plan, lax.axis_size("lo"), CHUNKS, leaves.shape[1]),
        out_shape=jax.ShapeDtypeStruct(vectors.shape, vectors.dtype),
        in_specs=[pl.BlockSpec(memory_space=pl.ANY)] * 6,
        out_specs=pl.BlockSpec(memory_space=pltpu.VMEM),
        scratch_shapes=scratch,
        compiler_params=pltpu.CompilerParams(
            collective_id=0, has_side_effects=True, vmem_limit_bytes=56 * 2**20
        ),
    )(vectors, leaves, u_local, v_local, u_upper, v_upper)


def solution(mesh):
    return jax.shard_map(
        local,
        mesh=mesh,
        in_specs=(
            P(None, ("hi", "lo")),
            P(("hi", "lo"), None),
            P(None, ("hi", "lo"), None),
            P(None, ("hi", "lo"), None),
            P(None, ("hi", "lo"), None),
            P(None, ("hi", "lo"), None),
        ),
        out_specs=P(None, ("hi", "lo")),
        check_vma=False,
    )
```

```python
import functools
import math

import jax
import jax.numpy as jnp
from jax import lax
from jax.experimental import pallas as pl
from jax.experimental.pallas import tpu as pltpu
from jax.sharding import PartitionSpec as P

ITERS = 4
GROUP_BITS = 2
CHUNKS = 2
MESH = pl.DeviceIdType.MESH
F32 = jnp.float32
BF16 = jnp.bfloat16


def flip(value, mask):
    bit = 0
    out = value
    while mask >> bit:
        if (mask >> bit) & 1:
            step = 2**bit
            out = out + step - 2 * step * lax.rem(lax.div(value, step), 2)
        bit += 1
    return out


class Plan:
    def __init__(self, levels, group_bits, wide):
        self.levels = levels
        self.k = min(group_bits, levels - 1)
        self.wide = wide
        k = self.k
        self.runs = [(b, 1, 2**b) for b in range(1, k)] + [(k, levels - k, 2**k)]
        self.first = [(r, m) for r, run in enumerate(self.runs) for m in range(1, run[2])]
        self.cross = [(b, m) for b in range(levels) for m in range(2 ** max(0, b - k))]
        self.slots2 = [(b, m) for b, m in self.cross if b > k]

    def rows(self, group):
        return self.wide // group

    def cross_mask(self, b, m):
        return (1 << b) ^ (m << self.k)

    def partners(self):
        masks = {m for _, m in self.first} | {self.cross_mask(b, m) for b, m in self.cross}
        return sorted(masks)


def nt(a, b):
    return lax.dot_general(a, b, (((1,), (1,)), ((), ())), preferred_element_type=F32)


def nn(a, b):
    return jnp.dot(a, b, preferred_element_type=F32)


def kernel(plan, lo_size, chunks, leaf_rows, *refs):
    hbm, o_ref = refs[:6], refs[6]
    leaves, u_loc, v_loc, u_up, v_up = refs[7:12]
    acc, parts, coef, recv2 = refs[12:16]
    recv1 = refs[16 : 16 + len(plan.runs)]
    load_sem, s1, r1, s2, r2, s3, r3 = refs[16 + len(plan.runs) :]
    levels, k = plan.levels, plan.k
    wide = plan.wide
    dev_rows = o_ref.shape[1]
    local_count = u_loc.shape[0]
    level_count = local_count + levels
    leaf_count = dev_rows // leaf_rows
    lo_bits = lo_size.bit_length() - 1

    dests = (o_ref, leaves, u_loc, v_loc, u_up, v_up)
    loads = [pltpu.make_async_copy(hbm[i], dests[i], load_sem.at[i]) for i in range(6)]
    for i in (0, 5, 1, 3, 2, 4):
        loads[i].start()

    hi = lax.axis_index("hi")
    lo = lax.axis_index("lo")
    me = hi * lo_size + lo

    def peer(mask):
        return (flip(hi, mask >> lo_bits), flip(lo, mask & (lo_size - 1)))

    barrier = pltpu.get_barrier_semaphore()
    masks = plan.partners()
    for mask in masks:
        pl.semaphore_signal(barrier, inc=1, device_id=peer(mask), device_id_type=MESH)
    loads[0].wait()
    loads[5].wait()
    pl.semaphore_wait(barrier, len(masks))

    def piece(group, mask):
        rows = plan.rows(group)
        index = flip(lax.rem(me, group), mask)
        return pl.ds(pl.multiple_of(index * rows, 8), rows)

    def copy1(slot, i):
        run, m = plan.first[i]
        b, count, group = plan.runs[run]
        return pltpu.make_async_remote_copy(
            src_ref=parts.at[slot, pl.ds(b, count), piece(group, m)],
            dst_ref=recv1[run].at[slot, m - 1],
            send_sem=s1.at[slot, i],
            recv_sem=r1.at[slot, i],
            device_id=peer(m),
            device_id_type=MESH,
        )

    def copy2(slot, i):
        b, m = plan.cross[i]
        mine = piece(2 ** min(b, k), 0)
        if b > k:
            target = recv2.at[slot, plan.slots2.index((b, m))]
        else:
            target = coef.at[slot, b, mine]
        return pltpu.make_async_remote_copy(
            src_ref=parts.at[slot, b, mine],
            dst_ref=target,
            send_sem=s2.at[slot, i],
            recv_sem=r2.at[slot, i],
            device_id=peer(plan.cross_mask(b, m)),
            device_id_type=MESH,
        )

    def copy3(slot, i):
        run, m = plan.first[i]
        b, count, group = plan.runs[run]
        mine = coef.at[slot, pl.ds(b, count), piece(group, 0)]
        return pltpu.make_async_remote_copy(
            src_ref=mine,
            dst_ref=mine,
            send_sem=s3.at[slot, i],
            recv_sem=r3.at[slot, i],
            device_id=peer(m),
            device_id_type=MESH,
        )

    def factor(node_rows):
        return 1.0 / math.sqrt(node_rows * level_count)

    def leaf_slice(g):
        return slice(g * leaf_rows, (g + 1) * leaf_rows)

    def project(slot, c):
        me_rows = slice(c * wide, (c + 1) * wide)
        top = levels
        while top > 0:
            low = max(top - 2, 0)
            group = list(range(low, top))
            total = None
            for g in range(leaf_count):
                cols = leaf_slice(g)
                weights = jnp.concatenate([v_up[b, cols, :] for b in group], axis=1)
                term = nn(o_ref[me_rows, cols], weights)
                total = term if total is None else total + term
            rank = total.shape[1] // len(group)
            for i, b in enumerate(group):
                parts[slot, b] = total[:, i * rank : (i + 1) * rank]
            for i, (run, m) in enumerate(plan.first):
                if low <= plan.runs[run][0] < top:
                    copy1(slot, i).start()
            top = low

    def local_part(slot, c):
        me_rows = slice(c * wide, (c + 1) * wide)
        sums = []
        for g in range(leaf_count):
            cols = leaf_slice(g)
            weights = jnp.concatenate([v_loc[j, cols, :] for j in range(local_count)], axis=1)
            sums.append(nn(o_ref[me_rows, cols], weights))
        rank = sums[0].shape[1] // local_count
        for g in range(leaf_count):
            cols = leaf_slice(g)
            pieces = []
            for j in range(local_count):
                node = (g >> j) ^ 1
                total = None
                for h in range(node << j, (node + 1) << j):
                    term = sums[h][:, j * rank : (j + 1) * rank]
                    total = term if total is None else total + term
                pieces.append((total * factor(leaf_rows * 2**j)).astype(BF16))
            bases = jnp.concatenate([u_loc[j, cols, :] for j in range(local_count)], axis=1)
            acc[me_rows, cols] = nt(o_ref[me_rows, cols], leaves[cols, :]) + nt(
                jnp.concatenate(pieces, axis=1), bases
            )

    def reduce_send(slot):
        for run, (b, count, group) in enumerate(plan.runs):
            for i, (r, m) in enumerate(plan.first):
                if r == run:
                    copy1(slot, i).wait_recv()
            mine = piece(group, 0)
            total = parts[slot, pl.ds(b, count), mine, :]
            for m in range(1, group):
                total = total + recv1[run][slot, m - 1]
            parts[slot, pl.ds(b, count), mine, :] = total
            for i, (level, m) in enumerate(plan.cross):
                if b <= level < b + count:
                    copy2(slot, i).start()
        for i, (level, m) in enumerate(plan.cross):
            if level == 0:
                copy2(slot, i).start()

    def cross_send(slot):
        for run, (b, count, group) in enumerate(plan.runs):
            for level in range(b, b + count):
                total = None
                for i, (other, m) in enumerate(plan.cross):
                    if other == level:
                        copy2(slot, i).wait_recv()
                        if level > k:
                            term = recv2[slot, plan.slots2.index((level, m))]
                            total = term if total is None else total + term
                if total is not None:
                    coef[slot, level, piece(group, 0), :] = total
            for i, (r, m) in enumerate(plan.first):
                if r == run:
                    copy3(slot, i).start()

    def finish(slot, c):
        me_rows = slice(c * wide, (c + 1) * wide)
        for i, (b, m) in enumerate(plan.cross):
            if b == 0:
                copy2(slot, i).wait_recv()
        for i in range(len(plan.first)):
            copy3(slot, i).wait_recv()
        scaled = jnp.concatenate(
            [(coef[slot, b] * factor(dev_rows * 2**b)).astype(BF16) for b in range(levels)],
            axis=1,
        )
        for g in range(leaf_count):
            cols = leaf_slice(g)
            bases = jnp.concatenate([u_up[b, cols, :] for b in range(levels)], axis=1)
            o_ref[me_rows, cols] = (acc[me_rows, cols] + nt(scaled, bases)).astype(BF16)

    def drain(slot, carry):
        for i in range(len(plan.first)):
            copy1(slot, i).wait_send()
            copy3(slot, i).wait_send()
        for i in range(len(plan.cross)):
            copy2(slot, i).wait_send()
        return carry

    def body(it, carry):
        slots = [it * chunks + c for c in range(chunks)]

        @pl.when(it == 0)
        def _():
            for i in (1, 2, 3):
                loads[i].wait()

        for c in range(chunks):
            local_part(slots[c], c)
            reduce_send(slots[c])
        for c in range(chunks):
            cross_send(slots[c])

        @pl.when(it == 0)
        def _():
            loads[4].wait()

        for c in range(chunks):
            finish(slots[c], c)

            @pl.when(it < ITERS - 1)
            def _():
                project(slots[c] + chunks, c)

        return carry

    for c in range(chunks):
        project(c, c)
    lax.fori_loop(0, ITERS, body, 0)
    lax.fori_loop(0, ITERS * chunks, drain, 0)


def local(vectors, leaves, u_local, v_local, u_upper, v_upper):
    wide = vectors.shape[0]
    levels = u_upper.shape[0]
    rank = u_upper.shape[2]
    plan = Plan(levels, GROUP_BITS, wide // CHUNKS)
    slots = ITERS * CHUNKS
    n1, n2 = len(plan.first), len(plan.cross)
    big = plan.rows(2**plan.k)
    dma = pltpu.SemaphoreType.DMA
    scratch = [pltpu.VMEM(x.shape, x.dtype) for x in (leaves, u_local, v_local, u_upper, v_upper)]
    scratch += [
        pltpu.VMEM(vectors.shape, F32),
        pltpu.VMEM((slots, levels, plan.wide, rank), F32),
        pltpu.VMEM((slots, levels, plan.wide, rank), F32),
        pltpu.VMEM((slots, max(1, len(plan.slots2)), big, rank), F32),
    ]
    scratch += [
        pltpu.VMEM((slots, group - 1, count, plan.rows(group), rank), F32)
        for _, count, group in plan.runs
    ]
    scratch += [dma((6,)), dma((slots, n1)), dma((slots, n1)), dma((slots, n2)), dma((slots, n2))]
    scratch += [dma((slots, n1)), dma((slots, n1))]
    return pl.pallas_call(
        functools.partial(kernel, plan, lax.axis_size("lo"), CHUNKS, leaves.shape[1]),
        out_shape=jax.ShapeDtypeStruct(vectors.shape, vectors.dtype),
        in_specs=[pl.BlockSpec(memory_space=pl.ANY)] * 6,
        out_specs=pl.BlockSpec(memory_space=pltpu.VMEM),
        scratch_shapes=scratch,
        compiler_params=pltpu.CompilerParams(
            collective_id=0, has_side_effects=True, vmem_limit_bytes=56 * 2**20
        ),
    )(vectors, leaves, u_local, v_local, u_upper, v_upper)


def solution(mesh):
    return jax.shard_map(
        local,
        mesh=mesh,
        in_specs=(
            P(None, ("hi", "lo")),
            P(("hi", "lo"), None),
            P(None, ("hi", "lo"), None),
            P(None, ("hi", "lo"), None),
            P(None, ("hi", "lo"), None),
            P(None, ("hi", "lo"), None),
        ),
        out_specs=P(None, ("hi", "lo")),
        check_vma=False,
    )
```

```python
import functools
import math

import jax
import jax.numpy as jnp
from jax import lax
from jax.experimental import pallas as pl
from jax.experimental.pallas import tpu as pltpu
from jax.sharding import PartitionSpec as P

ITERS = 4
CHUNKS = 2
MESH = pl.DeviceIdType.MESH
F32 = jnp.float32
BF16 = jnp.bfloat16


def flip(value, mask):
    bit = 0
    out = value
    while mask >> bit:
        if (mask >> bit) & 1:
            step = 2**bit
            out = out + step - 2 * step * lax.rem(lax.div(value, step), 2)
        bit += 1
    return out


def spread(index, bits):
    return sum(1 << bit for i, bit in enumerate(bits) if (index >> i) & 1)


def group_bits(level):
    if level >= 4:
        return (1, 2)
    return tuple(range(min(level, 2)))


class Plan:
    def __init__(self, levels, wide):
        self.levels = levels
        self.wide = wide
        self.runs = []
        for b in range(1, levels):
            if self.runs and self.runs[-1][2] == group_bits(b):
                first, count, bits = self.runs[-1]
                self.runs[-1] = (first, count + 1, bits)
            else:
                self.runs.append((b, 1, group_bits(b)))
        self.first = [
            (r, m) for r, run in enumerate(self.runs) for m in range(1, 2 ** len(run[2]))
        ]
        self.cross = [(b, m) for b in range(levels) for m in range(2 ** len(self.rest(b)))]
        self.slots2 = [(b, m) for b, m in self.cross if self.rest(b)]

    def rest(self, b):
        return [bit for bit in range(b) if bit not in group_bits(b)]

    def rows(self, bits):
        return self.wide // 2 ** len(bits)

    def first_mask(self, run, m):
        return spread(m, self.runs[run][2])

    def cross_mask(self, b, m):
        return (1 << b) ^ spread(m, self.rest(b))

    def partners(self):
        masks = {self.first_mask(r, m) for r, m in self.first}
        masks |= {self.cross_mask(b, m) for b, m in self.cross}
        return sorted(masks)


def nt(a, b):
    return lax.dot_general(a, b, (((1,), (1,)), ((), ())), preferred_element_type=F32)


def nn(a, b):
    return jnp.dot(a, b, preferred_element_type=F32)


def kernel(plan, lo_size, chunks, leaf_rows, *refs):
    hbm, o_ref = refs[:6], refs[6]
    leaves, u_loc, v_loc, u_up, v_up = refs[7:12]
    acc, parts, coef, recv2 = refs[12:16]
    recv1 = refs[16 : 16 + len(plan.runs)]
    load_sem, s1, r1, s2, r2, s3, r3 = refs[16 + len(plan.runs) :]
    levels = plan.levels
    wide = plan.wide
    dev_rows = o_ref.shape[1]
    local_count = u_loc.shape[0]
    level_count = local_count + levels
    leaf_count = dev_rows // leaf_rows
    lo_bits = lo_size.bit_length() - 1

    dests = (o_ref, leaves, u_loc, v_loc, u_up, v_up)
    loads = [pltpu.make_async_copy(hbm[i], dests[i], load_sem.at[i]) for i in range(6)]
    for i in (0, 5, 1, 3, 2, 4):
        loads[i].start()

    hi = lax.axis_index("hi")
    lo = lax.axis_index("lo")
    me = hi * lo_size + lo

    def peer(mask):
        return (flip(hi, mask >> lo_bits), flip(lo, mask & (lo_size - 1)))

    barrier = pltpu.get_barrier_semaphore()
    masks = plan.partners()
    for mask in masks:
        pl.semaphore_signal(barrier, inc=1, device_id=peer(mask), device_id_type=MESH)
    loads[0].wait()
    loads[5].wait()
    pl.semaphore_wait(barrier, len(masks))

    def piece(bits, mask):
        rows = plan.rows(bits)
        index = 0
        for i, bit in enumerate(bits):
            index = index + lax.rem(lax.div(me, 2**bit), 2) * 2**i
        if not bits:
            return pl.ds(0, rows)
        return pl.ds(pl.multiple_of(flip(index, mask) * rows, 8), rows)

    def copy1(slot, i):
        run, m = plan.first[i]
        b, count, bits = plan.runs[run]
        return pltpu.make_async_remote_copy(
            src_ref=parts.at[slot, pl.ds(b, count), piece(bits, m)],
            dst_ref=recv1[run].at[slot, m - 1],
            send_sem=s1.at[slot, i],
            recv_sem=r1.at[slot, i],
            device_id=peer(plan.first_mask(run, m)),
            device_id_type=MESH,
        )

    def copy2(slot, i):
        b, m = plan.cross[i]
        mine = piece(group_bits(b), 0)
        if plan.rest(b):
            target = recv2.at[slot, plan.slots2.index((b, m))]
        else:
            target = coef.at[slot, b, mine]
        return pltpu.make_async_remote_copy(
            src_ref=parts.at[slot, b, mine],
            dst_ref=target,
            send_sem=s2.at[slot, i],
            recv_sem=r2.at[slot, i],
            device_id=peer(plan.cross_mask(b, m)),
            device_id_type=MESH,
        )

    def copy3(slot, i):
        run, m = plan.first[i]
        b, count, bits = plan.runs[run]
        mine = coef.at[slot, pl.ds(b, count), piece(bits, 0)]
        return pltpu.make_async_remote_copy(
            src_ref=mine,
            dst_ref=mine,
            send_sem=s3.at[slot, i],
            recv_sem=r3.at[slot, i],
            device_id=peer(plan.first_mask(run, m)),
            device_id_type=MESH,
        )

    def factor(node_rows):
        return 1.0 / math.sqrt(node_rows * level_count)

    def leaf_slice(g):
        return slice(g * leaf_rows, (g + 1) * leaf_rows)

    def project(slot, c):
        me_rows = slice(c * wide, (c + 1) * wide)
        top = levels
        while top > 0:
            low = max(top - 2, 0)
            group = list(range(low, top))
            total = None
            for g in range(leaf_count):
                cols = leaf_slice(g)
                weights = jnp.concatenate([v_up[b, cols, :] for b in group], axis=1)
                term = nn(o_ref[me_rows, cols], weights)
                total = term if total is None else total + term
            rank = total.shape[1] // len(group)
            for i, b in enumerate(group):
                parts[slot, b] = total[:, i * rank : (i + 1) * rank]
            for i, (run, m) in enumerate(plan.first):
                if low <= plan.runs[run][0] < top:
                    copy1(slot, i).start()
            top = low

    def local_part(slot, c):
        me_rows = slice(c * wide, (c + 1) * wide)
        sums = []
        for g in range(leaf_count):
            cols = leaf_slice(g)
            weights = jnp.concatenate([v_loc[j, cols, :] for j in range(local_count)], axis=1)
            sums.append(nn(o_ref[me_rows, cols], weights))
        rank = sums[0].shape[1] // local_count
        for g in range(leaf_count):
            cols = leaf_slice(g)
            pieces = []
            for j in range(local_count):
                node = (g >> j) ^ 1
                total = None
                for h in range(node << j, (node + 1) << j):
                    term = sums[h][:, j * rank : (j + 1) * rank]
                    total = term if total is None else total + term
                pieces.append((total * factor(leaf_rows * 2**j)).astype(BF16))
            bases = jnp.concatenate([u_loc[j, cols, :] for j in range(local_count)], axis=1)
            acc[me_rows, cols] = nt(o_ref[me_rows, cols], leaves[cols, :]) + nt(
                jnp.concatenate(pieces, axis=1), bases
            )

    def reduce_send(slot):
        for run, (b, count, bits) in reversed(list(enumerate(plan.runs))):
            for i, (r, m) in enumerate(plan.first):
                if r == run:
                    copy1(slot, i).wait_recv()
            mine = piece(bits, 0)
            total = parts[slot, pl.ds(b, count), mine, :]
            for m in range(1, 2 ** len(bits)):
                total = total + recv1[run][slot, m - 1]
            parts[slot, pl.ds(b, count), mine, :] = total
            for i, (level, m) in enumerate(plan.cross):
                if b <= level < b + count:
                    copy2(slot, i).start()
        for i, (level, m) in enumerate(plan.cross):
            if level == 0:
                copy2(slot, i).start()

    def cross_send(slot):
        for run, (b, count, bits) in enumerate(plan.runs):
            for level in range(b, b + count):
                total = None
                for i, (other, m) in enumerate(plan.cross):
                    if other == level:
                        copy2(slot, i).wait_recv()
                        if plan.rest(level):
                            term = recv2[slot, plan.slots2.index((level, m))]
                            total = term if total is None else total + term
                if total is not None:
                    coef[slot, level, piece(bits, 0), :] = total
            for i, (r, m) in enumerate(plan.first):
                if r == run:
                    copy3(slot, i).start()

    def finish(slot, c):
        me_rows = slice(c * wide, (c + 1) * wide)
        for i, (b, m) in enumerate(plan.cross):
            if b == 0:
                copy2(slot, i).wait_recv()
        for i in range(len(plan.first)):
            copy3(slot, i).wait_recv()
        scaled = jnp.concatenate(
            [(coef[slot, b] * factor(dev_rows * 2**b)).astype(BF16) for b in range(levels)],
            axis=1,
        )
        for g in range(leaf_count):
            cols = leaf_slice(g)
            bases = jnp.concatenate([u_up[b, cols, :] for b in range(levels)], axis=1)
            o_ref[me_rows, cols] = (acc[me_rows, cols] + nt(scaled, bases)).astype(BF16)

    def drain(slot, carry):
        for i in range(len(plan.first)):
            copy1(slot, i).wait_send()
            copy3(slot, i).wait_send()
        for i in range(len(plan.cross)):
            copy2(slot, i).wait_send()
        return carry

    def body(it, carry):
        slots = [it * chunks + c for c in range(chunks)]

        @pl.when(it == 0)
        def _():
            for i in (1, 2, 3):
                loads[i].wait()

        for c in range(chunks):
            local_part(slots[c], c)
            reduce_send(slots[c])
        for c in range(chunks):
            cross_send(slots[c])

        @pl.when(it == 0)
        def _():
            loads[4].wait()

        for c in range(chunks):
            finish(slots[c], c)

            @pl.when(it < ITERS - 1)
            def _():
                project(slots[c] + chunks, c)

        return carry

    for c in range(chunks):
        project(c, c)
    lax.fori_loop(0, ITERS, body, 0)
    lax.fori_loop(0, ITERS * chunks, drain, 0)


def local(vectors, leaves, u_local, v_local, u_upper, v_upper):
    wide = vectors.shape[0]
    levels = u_upper.shape[0]
    rank = u_upper.shape[2]
    plan = Plan(levels, wide // CHUNKS)
    slots = ITERS * CHUNKS
    n1, n2 = len(plan.first), len(plan.cross)
    big = plan.rows(group_bits(levels))
    dma = pltpu.SemaphoreType.DMA
    scratch = [pltpu.VMEM(x.shape, x.dtype) for x in (leaves, u_local, v_local, u_upper, v_upper)]
    scratch += [
        pltpu.VMEM(vectors.shape, F32),
        pltpu.VMEM((slots, levels, plan.wide, rank), F32),
        pltpu.VMEM((slots, levels, plan.wide, rank), F32),
        pltpu.VMEM((slots, max(1, len(plan.slots2)), big, rank), F32),
    ]
    scratch += [
        pltpu.VMEM((slots, 2 ** len(bits) - 1, count, plan.rows(bits), rank), F32)
        for _, count, bits in plan.runs
    ]
    scratch += [dma((6,)), dma((slots, n1)), dma((slots, n1)), dma((slots, n2)), dma((slots, n2))]
    scratch += [dma((slots, n1)), dma((slots, n1))]
    return pl.pallas_call(
        functools.partial(kernel, plan, lax.axis_size("lo"), CHUNKS, leaves.shape[1]),
        out_shape=jax.ShapeDtypeStruct(vectors.shape, vectors.dtype),
        in_specs=[pl.BlockSpec(memory_space=pl.ANY)] * 6,
        out_specs=pl.BlockSpec(memory_space=pltpu.VMEM),
        scratch_shapes=scratch,
        compiler_params=pltpu.CompilerParams(
            collective_id=0, has_side_effects=True, vmem_limit_bytes=56 * 2**20
        ),
    )(vectors, leaves, u_local, v_local, u_upper, v_upper)


def solution(mesh):
    return jax.shard_map(
        local,
        mesh=mesh,
        in_specs=(
            P(None, ("hi", "lo")),
            P(("hi", "lo"), None),
            P(None, ("hi", "lo"), None),
            P(None, ("hi", "lo"), None),
            P(None, ("hi", "lo"), None),
            P(None, ("hi", "lo"), None),
        ),
        out_specs=P(None, ("hi", "lo")),
        check_vma=False,
    )
```

```python
import functools
import math

import jax
import jax.numpy as jnp
from jax import lax
from jax.experimental import pallas as pl
from jax.experimental.pallas import tpu as pltpu
from jax.sharding import PartitionSpec as P

ITERS = 4
CHUNKS = 2
MESH = pl.DeviceIdType.MESH
F32 = jnp.float32
BF16 = jnp.bfloat16


def flip(value, mask):
    bit = 0
    out = value
    while mask >> bit:
        if (mask >> bit) & 1:
            step = 2**bit
            out = out + step - 2 * step * lax.rem(lax.div(value, step), 2)
        bit += 1
    return out


def spread(index, bits):
    return sum(1 << bit for i, bit in enumerate(bits) if (index >> i) & 1)


def group_bits(level):
    if level >= 4:
        return (1, 2)
    return tuple(range(min(level, 2)))


class Plan:
    def __init__(self, levels, wide):
        self.levels = levels
        self.wide = wide
        self.runs = []
        for b in range(1, levels):
            if self.runs and self.runs[-1][2] == group_bits(b):
                first, count, bits = self.runs[-1]
                self.runs[-1] = (first, count + 1, bits)
            else:
                self.runs.append((b, 1, group_bits(b)))
        self.first = [
            (r, m) for r, run in enumerate(self.runs) for m in range(1, 2 ** len(run[2]))
        ]
        self.cross = [(b, m) for b in range(levels) for m in range(2 ** len(self.rest(b)))]
        self.slots2 = [(b, m) for b, m in self.cross if self.rest(b)]

    def rest(self, b):
        return [bit for bit in range(b) if bit not in group_bits(b)]

    def rows(self, bits):
        return self.wide // 2 ** len(bits)

    def first_mask(self, run, m):
        return spread(m, self.runs[run][2])

    def cross_mask(self, b, m):
        return (1 << b) ^ spread(m, self.rest(b))

    def partners(self):
        masks = {self.first_mask(r, m) for r, m in self.first}
        masks |= {self.cross_mask(b, m) for b, m in self.cross}
        return sorted(masks)


def nn(a, b):
    return jnp.dot(a, b, preferred_element_type=F32)


def kernel(plan, lo_size, chunks, leaf_rows, *refs):
    hbm, o_ref = refs[:6], refs[6]
    leaves, u_loc, v_loc, u_up, v_up = refs[7:12]
    acc, parts, coef, recv2 = refs[12:16]
    leaves_t, u_loc_t, u_up_t = refs[16:19]
    recv1 = refs[19 : 19 + len(plan.runs)]
    load_sem, s1, r1, s2, r2, s3, r3 = refs[19 + len(plan.runs) :]
    levels = plan.levels
    wide = plan.wide
    dev_rows = o_ref.shape[1]
    local_count = u_loc.shape[0]
    level_count = local_count + levels
    leaf_count = dev_rows // leaf_rows
    lo_bits = lo_size.bit_length() - 1

    dests = (o_ref, leaves, u_loc, v_loc, u_up, v_up)
    loads = [pltpu.make_async_copy(hbm[i], dests[i], load_sem.at[i]) for i in range(6)]
    for i in (0, 5, 1, 3, 2, 4):
        loads[i].start()

    hi = lax.axis_index("hi")
    lo = lax.axis_index("lo")
    me = hi * lo_size + lo

    def peer(mask):
        return (flip(hi, mask >> lo_bits), flip(lo, mask & (lo_size - 1)))

    barrier = pltpu.get_barrier_semaphore()
    masks = plan.partners()
    for mask in masks:
        pl.semaphore_signal(barrier, inc=1, device_id=peer(mask), device_id_type=MESH)
    loads[0].wait()
    loads[5].wait()
    pl.semaphore_wait(barrier, len(masks))

    def piece(bits, mask):
        rows = plan.rows(bits)
        index = 0
        for i, bit in enumerate(bits):
            index = index + lax.rem(lax.div(me, 2**bit), 2) * 2**i
        if not bits:
            return pl.ds(0, rows)
        return pl.ds(pl.multiple_of(flip(index, mask) * rows, 8), rows)

    def copy1(slot, i):
        run, m = plan.first[i]
        b, count, bits = plan.runs[run]
        return pltpu.make_async_remote_copy(
            src_ref=parts.at[slot, pl.ds(b, count), piece(bits, m)],
            dst_ref=recv1[run].at[slot, m - 1],
            send_sem=s1.at[slot, i],
            recv_sem=r1.at[slot, i],
            device_id=peer(plan.first_mask(run, m)),
            device_id_type=MESH,
        )

    def copy2(slot, i):
        b, m = plan.cross[i]
        mine = piece(group_bits(b), 0)
        if plan.rest(b):
            target = recv2.at[slot, plan.slots2.index((b, m))]
        else:
            target = coef.at[slot, b, mine]
        return pltpu.make_async_remote_copy(
            src_ref=parts.at[slot, b, mine],
            dst_ref=target,
            send_sem=s2.at[slot, i],
            recv_sem=r2.at[slot, i],
            device_id=peer(plan.cross_mask(b, m)),
            device_id_type=MESH,
        )

    def copy3(slot, i):
        run, m = plan.first[i]
        b, count, bits = plan.runs[run]
        mine = coef.at[slot, pl.ds(b, count), piece(bits, 0)]
        return pltpu.make_async_remote_copy(
            src_ref=mine,
            dst_ref=mine,
            send_sem=s3.at[slot, i],
            recv_sem=r3.at[slot, i],
            device_id=peer(plan.first_mask(run, m)),
            device_id_type=MESH,
        )

    def factor(node_rows):
        return 1.0 / math.sqrt(node_rows * level_count)

    def leaf_slice(g):
        return slice(g * leaf_rows, (g + 1) * leaf_rows)

    def turn(source, target):
        rank = source.shape[2]
        for b in range(source.shape[0]):
            for g in range(leaf_count):
                cols = leaf_slice(g)
                target[b * rank : (b + 1) * rank, cols] = source[b, cols, :].T

    def project(slot, c):
        me_rows = slice(c * wide, (c + 1) * wide)
        top = levels
        while top > 0:
            low = max(top - 2, 0)
            group = list(range(low, top))
            total = None
            for g in range(leaf_count):
                cols = leaf_slice(g)
                weights = jnp.concatenate([v_up[b, cols, :] for b in group], axis=1)
                term = nn(o_ref[me_rows, cols], weights)
                total = term if total is None else total + term
            rank = total.shape[1] // len(group)
            for i, b in enumerate(group):
                parts[slot, b] = total[:, i * rank : (i + 1) * rank]
            for i, (run, m) in enumerate(plan.first):
                if low <= plan.runs[run][0] < top:
                    copy1(slot, i).start()
            top = low

    def local_part(slot, c):
        me_rows = slice(c * wide, (c + 1) * wide)
        sums = []
        for g in range(leaf_count):
            cols = leaf_slice(g)
            weights = jnp.concatenate([v_loc[j, cols, :] for j in range(local_count)], axis=1)
            sums.append(nn(o_ref[me_rows, cols], weights))
        rank = sums[0].shape[1] // local_count
        for g in range(leaf_count):
            cols = leaf_slice(g)
            pieces = []
            for j in range(local_count):
                node = (g >> j) ^ 1
                total = None
                for h in range(node << j, (node + 1) << j):
                    term = sums[h][:, j * rank : (j + 1) * rank]
                    total = term if total is None else total + term
                pieces.append((total * factor(leaf_rows * 2**j)).astype(BF16))
            acc[me_rows, cols] = nn(o_ref[me_rows, cols], leaves_t[:, cols]) + nn(
                jnp.concatenate(pieces, axis=1), u_loc_t[:, cols]
            )

    def reduce_send(slot):
        for run, (b, count, bits) in reversed(list(enumerate(plan.runs))):
            for i, (r, m) in enumerate(plan.first):
                if r == run:
                    copy1(slot, i).wait_recv()
            mine = piece(bits, 0)
            total = parts[slot, pl.ds(b, count), mine, :]
            for m in range(1, 2 ** len(bits)):
                total = total + recv1[run][slot, m - 1]
            parts[slot, pl.ds(b, count), mine, :] = total
            for i, (level, m) in enumerate(plan.cross):
                if b <= level < b + count:
                    copy2(slot, i).start()
        for i, (level, m) in enumerate(plan.cross):
            if level == 0:
                copy2(slot, i).start()

    def cross_send(slot):
        for run, (b, count, bits) in enumerate(plan.runs):
            for level in range(b, b + count):
                total = None
                for i, (other, m) in enumerate(plan.cross):
                    if other == level:
                        copy2(slot, i).wait_recv()
                        if plan.rest(level):
                            term = recv2[slot, plan.slots2.index((level, m))]
                            total = term if total is None else total + term
                if total is not None:
                    coef[slot, level, piece(bits, 0), :] = total
            for i, (r, m) in enumerate(plan.first):
                if r == run:
                    copy3(slot, i).start()

    def finish(slot, c):
        me_rows = slice(c * wide, (c + 1) * wide)
        for i, (b, m) in enumerate(plan.cross):
            if b == 0:
                copy2(slot, i).wait_recv()
        for i in range(len(plan.first)):
            copy3(slot, i).wait_recv()
        scaled = jnp.concatenate(
            [(coef[slot, b] * factor(dev_rows * 2**b)).astype(BF16) for b in range(levels)],
            axis=1,
        )
        for g in range(leaf_count):
            cols = leaf_slice(g)
            o_ref[me_rows, cols] = (acc[me_rows, cols] + nn(scaled, u_up_t[:, cols])).astype(BF16)

    def drain(slot, carry):
        for i in range(len(plan.first)):
            copy1(slot, i).wait_send()
            copy3(slot, i).wait_send()
        for i in range(len(plan.cross)):
            copy2(slot, i).wait_send()
        return carry

    def body(it, carry):
        slots = [it * chunks + c for c in range(chunks)]

        @pl.when(it == 0)
        def _():
            for i in (1, 2, 3):
                loads[i].wait()
            for g in range(leaf_count):
                cols = leaf_slice(g)
                leaves_t[:, cols] = leaves[cols, :].T
            turn(u_loc, u_loc_t)

        for c in range(chunks):
            local_part(slots[c], c)
            reduce_send(slots[c])
        for c in range(chunks):
            cross_send(slots[c])

        @pl.when(it == 0)
        def _():
            loads[4].wait()
            turn(u_up, u_up_t)

        for c in range(chunks):
            finish(slots[c], c)

            @pl.when(it < ITERS - 1)
            def _():
                project(slots[c] + chunks, c)

        return carry

    for c in range(chunks):
        project(c, c)
    lax.fori_loop(0, ITERS, body, 0)
    lax.fori_loop(0, ITERS * chunks, drain, 0)


def local(vectors, leaves, u_local, v_local, u_upper, v_upper):
    wide = vectors.shape[0]
    levels = u_upper.shape[0]
    rank = u_upper.shape[2]
    plan = Plan(levels, wide // CHUNKS)
    slots = ITERS * CHUNKS
    n1, n2 = len(plan.first), len(plan.cross)
    big = plan.rows(group_bits(levels))
    dma = pltpu.SemaphoreType.DMA
    scratch = [pltpu.VMEM(x.shape, x.dtype) for x in (leaves, u_local, v_local, u_upper, v_upper)]
    scratch += [
        pltpu.VMEM(vectors.shape, F32),
        pltpu.VMEM((slots, levels, plan.wide, rank), F32),
        pltpu.VMEM((slots, levels, plan.wide, rank), F32),
        pltpu.VMEM((slots, max(1, len(plan.slots2)), big, rank), F32),
    ]
    dev_rows = vectors.shape[1]
    scratch += [
        pltpu.VMEM((leaves.shape[1], dev_rows), BF16),
        pltpu.VMEM((u_local.shape[0] * rank, dev_rows), BF16),
        pltpu.VMEM((levels * rank, dev_rows), BF16),
    ]
    scratch += [
        pltpu.VMEM((slots, 2 ** len(bits) - 1, count, plan.rows(bits), rank), F32)
        for _, count, bits in plan.runs
    ]
    scratch += [dma((6,)), dma((slots, n1)), dma((slots, n1)), dma((slots, n2)), dma((slots, n2))]
    scratch += [dma((slots, n1)), dma((slots, n1))]
    return pl.pallas_call(
        functools.partial(kernel, plan, lax.axis_size("lo"), CHUNKS, leaves.shape[1]),
        out_shape=jax.ShapeDtypeStruct(vectors.shape, vectors.dtype),
        in_specs=[pl.BlockSpec(memory_space=pl.ANY)] * 6,
        out_specs=pl.BlockSpec(memory_space=pltpu.VMEM),
        scratch_shapes=scratch,
        compiler_params=pltpu.CompilerParams(
            collective_id=0, has_side_effects=True, vmem_limit_bytes=56 * 2**20
        ),
    )(vectors, leaves, u_local, v_local, u_upper, v_upper)


def solution(mesh):
    return jax.shard_map(
        local,
        mesh=mesh,
        in_specs=(
            P(None, ("hi", "lo")),
            P(("hi", "lo"), None),
            P(None, ("hi", "lo"), None),
            P(None, ("hi", "lo"), None),
            P(None, ("hi", "lo"), None),
            P(None, ("hi", "lo"), None),
        ),
        out_specs=P(None, ("hi", "lo")),
        check_vma=False,
    )
```

```python
import functools
import math

import jax
import jax.numpy as jnp
from jax import lax
from jax.experimental import pallas as pl
from jax.experimental.pallas import tpu as pltpu
from jax.sharding import PartitionSpec as P

ITERS = 4
CHUNKS = 1
MESH = pl.DeviceIdType.MESH
F32 = jnp.float32
BF16 = jnp.bfloat16


def flip(value, mask):
    bit = 0
    out = value
    while mask >> bit:
        if (mask >> bit) & 1:
            step = 2**bit
            out = out + step - 2 * step * lax.rem(lax.div(value, step), 2)
        bit += 1
    return out


def spread(index, bits):
    return sum(1 << bit for i, bit in enumerate(bits) if (index >> i) & 1)


def group_bits(level):
    if level >= 4:
        return (1, 2)
    return tuple(range(min(level, 2)))


class Plan:
    def __init__(self, levels, wide):
        self.levels = levels
        self.wide = wide
        self.runs = []
        for b in range(1, levels):
            if self.runs and self.runs[-1][2] == group_bits(b):
                first, count, bits = self.runs[-1]
                self.runs[-1] = (first, count + 1, bits)
            else:
                self.runs.append((b, 1, group_bits(b)))
        self.first = [
            (r, m) for r, run in enumerate(self.runs) for m in range(1, 2 ** len(run[2]))
        ]
        self.cross = [(b, m) for b in range(levels) for m in range(2 ** len(self.rest(b)))]
        self.slots2 = [(b, m) for b, m in self.cross if self.rest(b)]

    def rest(self, b):
        return [bit for bit in range(b) if bit not in group_bits(b)]

    def rows(self, bits):
        return self.wide // 2 ** len(bits)

    def first_mask(self, run, m):
        return spread(m, self.runs[run][2])

    def cross_mask(self, b, m):
        return (1 << b) ^ spread(m, self.rest(b))

    def partners(self):
        masks = {self.first_mask(r, m) for r, m in self.first}
        masks |= {self.cross_mask(b, m) for b, m in self.cross}
        return sorted(masks)


def nn(a, b):
    return jnp.dot(a, b, preferred_element_type=F32)


def kernel(plan, lo_size, chunks, leaf_rows, *refs):
    hbm, o_ref = refs[:6], refs[6]
    leaves, u_loc, v_loc, u_up, v_up = refs[7:12]
    acc, parts, coef, recv2 = refs[12:16]
    leaves_t, u_loc_t, u_up_t = refs[16:19]
    recv1 = refs[19 : 19 + len(plan.runs)]
    load_sem, s1, r1, s2, r2, s3, r3 = refs[19 + len(plan.runs) :]
    levels = plan.levels
    wide = plan.wide
    dev_rows = o_ref.shape[1]
    local_count = u_loc.shape[0]
    level_count = local_count + levels
    leaf_count = dev_rows // leaf_rows
    lo_bits = lo_size.bit_length() - 1

    dests = (o_ref, leaves, u_loc, v_loc, u_up, v_up)
    loads = [pltpu.make_async_copy(hbm[i], dests[i], load_sem.at[i]) for i in range(6)]
    for i in (0, 5, 1, 3, 2, 4):
        loads[i].start()

    hi = lax.axis_index("hi")
    lo = lax.axis_index("lo")
    me = hi * lo_size + lo

    def peer(mask):
        return (flip(hi, mask >> lo_bits), flip(lo, mask & (lo_size - 1)))

    barrier = pltpu.get_barrier_semaphore()
    masks = plan.partners()
    for mask in masks:
        pl.semaphore_signal(barrier, inc=1, device_id=peer(mask), device_id_type=MESH)
    loads[0].wait()
    loads[5].wait()
    pl.semaphore_wait(barrier, len(masks))

    def piece(bits, mask):
        rows = plan.rows(bits)
        index = 0
        for i, bit in enumerate(bits):
            index = index + lax.rem(lax.div(me, 2**bit), 2) * 2**i
        if not bits:
            return pl.ds(0, rows)
        return pl.ds(pl.multiple_of(flip(index, mask) * rows, 8), rows)

    def copy1(slot, i):
        run, m = plan.first[i]
        b, count, bits = plan.runs[run]
        return pltpu.make_async_remote_copy(
            src_ref=parts.at[slot, pl.ds(b, count), piece(bits, m)],
            dst_ref=recv1[run].at[slot, m - 1],
            send_sem=s1.at[slot, i],
            recv_sem=r1.at[slot, i],
            device_id=peer(plan.first_mask(run, m)),
            device_id_type=MESH,
        )

    def copy2(slot, i):
        b, m = plan.cross[i]
        mine = piece(group_bits(b), 0)
        if plan.rest(b):
            target = recv2.at[slot, plan.slots2.index((b, m))]
        else:
            target = coef.at[slot, b, mine]
        return pltpu.make_async_remote_copy(
            src_ref=parts.at[slot, b, mine],
            dst_ref=target,
            send_sem=s2.at[slot, i],
            recv_sem=r2.at[slot, i],
            device_id=peer(plan.cross_mask(b, m)),
            device_id_type=MESH,
        )

    def copy3(slot, i):
        run, m = plan.first[i]
        b, count, bits = plan.runs[run]
        mine = coef.at[slot, pl.ds(b, count), piece(bits, 0)]
        return pltpu.make_async_remote_copy(
            src_ref=mine,
            dst_ref=mine,
            send_sem=s3.at[slot, i],
            recv_sem=r3.at[slot, i],
            device_id=peer(plan.first_mask(run, m)),
            device_id_type=MESH,
        )

    def factor(node_rows):
        return 1.0 / math.sqrt(node_rows * level_count)

    def leaf_slice(g):
        return slice(g * leaf_rows, (g + 1) * leaf_rows)

    def turn(source, target):
        rank = source.shape[2]
        for b in range(source.shape[0]):
            for g in range(leaf_count):
                cols = leaf_slice(g)
                target[b * rank : (b + 1) * rank, cols] = source[b, cols, :].T

    def project(slot, c):
        me_rows = slice(c * wide, (c + 1) * wide)
        top = levels
        while top > 0:
            low = max(top - 2, 0)
            group = list(range(low, top))
            total = None
            for g in range(leaf_count):
                cols = leaf_slice(g)
                weights = jnp.concatenate([v_up[b, cols, :] for b in group], axis=1)
                term = nn(o_ref[me_rows, cols], weights)
                total = term if total is None else total + term
            rank = total.shape[1] // len(group)
            for i, b in enumerate(group):
                parts[slot, b] = total[:, i * rank : (i + 1) * rank]
            for i, (run, m) in enumerate(plan.first):
                if low <= plan.runs[run][0] < top:
                    copy1(slot, i).start()
            top = low

    def local_part(slot, c):
        me_rows = slice(c * wide, (c + 1) * wide)
        sums = []
        for g in range(leaf_count):
            cols = leaf_slice(g)
            weights = jnp.concatenate([v_loc[j, cols, :] for j in range(local_count)], axis=1)
            sums.append(nn(o_ref[me_rows, cols], weights))
        rank = sums[0].shape[1] // local_count
        for g in range(leaf_count):
            cols = leaf_slice(g)
            pieces = []
            for j in range(local_count):
                node = (g >> j) ^ 1
                total = None
                for h in range(node << j, (node + 1) << j):
                    term = sums[h][:, j * rank : (j + 1) * rank]
                    total = term if total is None else total + term
                pieces.append((total * factor(leaf_rows * 2**j)).astype(BF16))
            acc[me_rows, cols] = nn(o_ref[me_rows, cols], leaves_t[:, cols]) + nn(
                jnp.concatenate(pieces, axis=1), u_loc_t[:, cols]
            )

    def reduce_send(slot):
        for run, (b, count, bits) in reversed(list(enumerate(plan.runs))):
            for i, (r, m) in enumerate(plan.first):
                if r == run:
                    copy1(slot, i).wait_recv()
            mine = piece(bits, 0)
            total = parts[slot, pl.ds(b, count), mine, :]
            for m in range(1, 2 ** len(bits)):
                total = total + recv1[run][slot, m - 1]
            parts[slot, pl.ds(b, count), mine, :] = total
            for i, (level, m) in enumerate(plan.cross):
                if b <= level < b + count:
                    copy2(slot, i).start()
        for i, (level, m) in enumerate(plan.cross):
            if level == 0:
                copy2(slot, i).start()

    def cross_send(slot):
        for run, (b, count, bits) in enumerate(plan.runs):
            for level in range(b, b + count):
                total = None
                for i, (other, m) in enumerate(plan.cross):
                    if other == level:
                        copy2(slot, i).wait_recv()
                        if plan.rest(level):
                            term = recv2[slot, plan.slots2.index((level, m))]
                            total = term if total is None else total + term
                if total is not None:
                    coef[slot, level, piece(bits, 0), :] = total
            for i, (r, m) in enumerate(plan.first):
                if r == run:
                    copy3(slot, i).start()

    def finish(slot, c):
        me_rows = slice(c * wide, (c + 1) * wide)
        for i, (b, m) in enumerate(plan.cross):
            if b == 0:
                copy2(slot, i).wait_recv()
        for i in range(len(plan.first)):
            copy3(slot, i).wait_recv()
        scaled = jnp.concatenate(
            [(coef[slot, b] * factor(dev_rows * 2**b)).astype(BF16) for b in range(levels)],
            axis=1,
        )
        for g in range(leaf_count):
            cols = leaf_slice(g)
            o_ref[me_rows, cols] = (acc[me_rows, cols] + nn(scaled, u_up_t[:, cols])).astype(BF16)

    def drain(slot, carry):
        for i in range(len(plan.first)):
            copy1(slot, i).wait_send()
            copy3(slot, i).wait_send()
        for i in range(len(plan.cross)):
            copy2(slot, i).wait_send()
        return carry

    def body(it, carry):
        slots = [it * chunks + c for c in range(chunks)]

        @pl.when(it == 0)
        def _():
            for i in (1, 2, 3):
                loads[i].wait()
            for g in range(leaf_count):
                cols = leaf_slice(g)
                leaves_t[:, cols] = leaves[cols, :].T
            turn(u_loc, u_loc_t)

        for c in range(chunks):
            local_part(slots[c], c)
            reduce_send(slots[c])
        for c in range(chunks):
            cross_send(slots[c])

        @pl.when(it == 0)
        def _():
            loads[4].wait()
            turn(u_up, u_up_t)

        for c in range(chunks):
            finish(slots[c], c)

            @pl.when(it < ITERS - 1)
            def _():
                project(slots[c] + chunks, c)

        return carry

    for c in range(chunks):
        project(c, c)
    lax.fori_loop(0, ITERS, body, 0)
    lax.fori_loop(0, ITERS * chunks, drain, 0)


def local(vectors, leaves, u_local, v_local, u_upper, v_upper):
    wide = vectors.shape[0]
    levels = u_upper.shape[0]
    rank = u_upper.shape[2]
    plan = Plan(levels, wide // CHUNKS)
    slots = ITERS * CHUNKS
    n1, n2 = len(plan.first), len(plan.cross)
    big = plan.rows(group_bits(levels))
    dma = pltpu.SemaphoreType.DMA
    scratch = [pltpu.VMEM(x.shape, x.dtype) for x in (leaves, u_local, v_local, u_upper, v_upper)]
    scratch += [
        pltpu.VMEM(vectors.shape, F32),
        pltpu.VMEM((slots, levels, plan.wide, rank), F32),
        pltpu.VMEM((slots, levels, plan.wide, rank), F32),
        pltpu.VMEM((slots, max(1, len(plan.slots2)), big, rank), F32),
    ]
    dev_rows = vectors.shape[1]
    scratch += [
        pltpu.VMEM((leaves.shape[1], dev_rows), BF16),
        pltpu.VMEM((u_local.shape[0] * rank, dev_rows), BF16),
        pltpu.VMEM((levels * rank, dev_rows), BF16),
    ]
    scratch += [
        pltpu.VMEM((slots, 2 ** len(bits) - 1, count, plan.rows(bits), rank), F32)
        for _, count, bits in plan.runs
    ]
    scratch += [dma((6,)), dma((slots, n1)), dma((slots, n1)), dma((slots, n2)), dma((slots, n2))]
    scratch += [dma((slots, n1)), dma((slots, n1))]
    return pl.pallas_call(
        functools.partial(kernel, plan, lax.axis_size("lo"), CHUNKS, leaves.shape[1]),
        out_shape=jax.ShapeDtypeStruct(vectors.shape, vectors.dtype),
        in_specs=[pl.BlockSpec(memory_space=pl.ANY)] * 6,
        out_specs=pl.BlockSpec(memory_space=pltpu.VMEM),
        scratch_shapes=scratch,
        compiler_params=pltpu.CompilerParams(
            collective_id=0, has_side_effects=True, vmem_limit_bytes=56 * 2**20
        ),
    )(vectors, leaves, u_local, v_local, u_upper, v_upper)


def solution(mesh):
    return jax.shard_map(
        local,
        mesh=mesh,
        in_specs=(
            P(None, ("hi", "lo")),
            P(("hi", "lo"), None),
            P(None, ("hi", "lo"), None),
            P(None, ("hi", "lo"), None),
            P(None, ("hi", "lo"), None),
            P(None, ("hi", "lo"), None),
        ),
        out_specs=P(None, ("hi", "lo")),
        check_vma=False,
    )
```
